32 devices in a mesh: row: 8 (over z, y), col: 2 (over x), tp: 2 (over core).
Axes of the slice: x: 2, y: 2, z: 4, core: 2. Of those that a mesh axis runs over, the one named last changes fastest.
Arguments:
- gram: float32 [16, 8, 128, 8, 2, 1024], P(None, 'row', 'tp', None, 'col'), may hold values from -24 to 24
- inv_factor: bfloat16 [1024, 1024], replicated, as said below
- cross_gram: bfloat16 [16, 8, 128, 1024], P(None, 'row', 'tp'), may hold values from -24 to 24
- down_rows: bfloat16 [29568, 4096], P(('row', 'tp'), 'col'), may hold values from -0.03125 to 0.03125
- removed: int32 [1024], replicated, may hold values from 0 to 29567, as said below
Outputs:
- updated: float32 [16, 8, 128, 8, 2, 1024], P(None, 'row', 'tp', None, 'col')
- rhs_next: float32 [16, 8, 128, 4096], P(None, 'row', 'tp', 'col')
The draws below stay inside these ranges and needn't reach their ends.
Inputs may be any that keep to these rules, and one draw needn't show every extreme that they name: `inv_factor`: zero above the diagonal. `removed`: distinct ids in ascending order; among the neurons s * 1848 to (s + 1) * 1848 - 1 of any shard s at most 256 are listed, and one shard holds exactly 256.
All inputs are finite; a program needn't handle non-finite values.
Results may differ from the reference program's by a relative error of at most 0.0003.
Values may be sent and summed in bfloat16 or wider, within the bound.
No kernel may reach another device: no remote copies, remote signals or barrier semaphores. Data moves between devices by JAX's collectives and lax.ppermute only.
A program may use at most 256 MiB of HBM per device.

```python
import jax
import jax.numpy as jnp
from jax import lax

FF = 29568
NR = 1024
DW = 4096
NB = 128
P_SIZE = 1024
CB = 1024
RC = 16
CCYC = 8
SHARDS = 16
FS = 1848
CAP = 256
N_ROW = 8
N_COL = 2


def draw_inv_factor(key, part):
    values = jax.random.normal(key, (P_SIZE, P_SIZE), jnp.float32) * (0.176 / P_SIZE ** 0.5)
    lines = lax.broadcasted_iota(jnp.int32, (P_SIZE, P_SIZE), 0)
    places = lax.broadcasted_iota(jnp.int32, (P_SIZE, P_SIZE), 1)
    return jnp.where(places <= lines, values, 0.0).astype(jnp.bfloat16)


def draw_removed(key, part):
    key_hot, key_spots, key_pick = jax.random.split(key, 3)
    hottest = jax.random.randint(key_hot, (), 0, SHARDS)
    shard_keys = jax.random.split(key_spots, SHARDS)

    def spots_of(one_key):
        return jax.random.permutation(one_key, FS)[:CAP]
    spots = jax.vmap(spots_of)(shard_keys)
    order = (hottest + jnp.arange(SHARDS, dtype=jnp.int32)) % SHARDS
    neuron_ids = spots[order] + (order * FS)[:, None]
    others = neuron_ids[1:].reshape(-1)
    picked = jax.random.permutation(key_pick, (SHARDS - 1) * CAP)[:NR - CAP]
    chosen = jnp.concatenate([neuron_ids[0], others[picked]])
    return jnp.sort(chosen).astype(jnp.int32)


def shard_levels(key, dims, cuts, smallest, largest):
    factor_of, own = 1.0, jax.random.fold_in(key, 6)
    for dim, blocks in cuts:
        heights = jnp.exp(jax.random.uniform(jax.random.fold_in(own, dim), (blocks,), jnp.float32, smallest / len(cuts), largest / len(cuts)))
        factor_of = factor_of * jnp.repeat(heights, dims[dim] // blocks).reshape([-1 if axis == dim else 1 for axis in range(len(dims))])
    return factor_of


def centred(rng, shape, scale, limit, shards=(), held_as=jnp.bfloat16):
    entries = jax.random.normal(rng, shape, jnp.float32) * scale
    if len(shards) > 0:
        entries = shard_levels(rng, shape, shards, -0.22, 0.18) * entries
    return jnp.clip(entries, min=-limit, max=limit).astype(held_as)


def setup_inputs(seed: int = 0) -> dict:
    key_of = jax.random.split(jax.random.key(seed), 6)
    return {
        "gram": centred(key_of[0], (RC, N_ROW, NB, CCYC, N_COL, CB), 4.0, 24.0, ((1, 8), (2, 2), (4, 2)), jnp.float32),
        "inv_factor": draw_inv_factor(jax.random.fold_in(key_of[5], 71), 0),
        "cross_gram": centred(key_of[2], (RC, N_ROW, NB, NR), 4.0, 24.0, ((1, 8), (2, 2))),
        "down_rows": centred(key_of[3], (FF, DW), FF ** -0.5, 0.03125, ((0, 16), (1, 2))),
        "removed": draw_removed(jax.random.fold_in(key_of[5], 71), 0),
    }


def reference(gram, inv_factor, cross_gram, down_rows, removed):
    total = gram.shape[0] * gram.shape[1] * gram.shape[2]
    matrix = gram.reshape(total, total)
    factor = inv_factor.astype(jnp.float32)
    panel_factor = jnp.dot(matrix[:, :P_SIZE], factor.T, precision=lax.Precision.HIGHEST, preferred_element_type=jnp.float32)
    blocks = total // 1024 if total % 1024 == 0 else 1
    rows_each = total // blocks

    def update_block(index):
        start = (index * rows_each).astype(jnp.int32)
        stored = lax.dynamic_slice_in_dim(matrix, start, rows_each, 0)
        left = lax.dynamic_slice_in_dim(panel_factor, start, rows_each, 0)
        return stored - jnp.dot(left, panel_factor.T, precision=lax.Precision.HIGHEST, preferred_element_type=jnp.float32)

    updated = lax.map(update_block, jnp.arange(blocks, dtype=jnp.int32)).reshape(gram.shape)
    lost_rows = jnp.take(down_rows, removed.astype(jnp.int32), axis=0)
    cross = cross_gram.reshape(total, cross_gram.shape[3])
    rhs = jnp.dot(cross, lost_rows, preferred_element_type=jnp.float32)
    head = jnp.dot(factor, rhs[:P_SIZE], precision=lax.Precision.HIGHEST, preferred_element_type=jnp.float32)
    rhs_next = rhs - jnp.dot(panel_factor, head, precision=lax.Precision.HIGHEST, preferred_element_type=jnp.float32)
    return updated, rhs_next.reshape(cross_gram.shape[0], cross_gram.shape[1], cross_gram.shape[2], down_rows.shape[1])
```

```python
import functools

import jax
import jax.numpy as jnp
from jax import lax
from jax.experimental import pallas as pl
from jax.experimental.pallas import tpu as pltpu
from jax.sharding import PartitionSpec as P

MEMBERS = ("far", "near", "tp")
LIMIT = 24.0
LEVELS = 32767.0
VMEM = 56 * 1024 * 1024

PIECES = ((0, 4), (4, 4))
STEP = 2


def encode(values):
    root = jnp.sqrt(jnp.abs(values)) * (LEVELS / LIMIT**0.5)
    code = jnp.clip(jnp.round(jnp.where(values < 0, -root, root)), -LEVELS, LEVELS).astype(jnp.int32)
    half = values.shape[-1] // 2
    return (code[..., :half] << 16) | (code[..., half:] & 0xFFFF)


def decode(words, factor):
    upper = (words >> 16).astype(jnp.float32)
    lower = ((words << 16) >> 16).astype(jnp.float32)
    return upper * (jnp.abs(upper) * factor), lower * (jnp.abs(lower) * factor)


def split(values):
    high = values.astype(jnp.bfloat16)
    return high, (values - high.astype(jnp.float32)).astype(jnp.bfloat16)


def solve_kernel(factor_ref, back_ref, words_ref, sh_ref, sl_ref, high_ref, low_ref):
    packed = words_ref.shape[1]
    total = None
    for half, values in enumerate(decode(words_ref[...], factor_ref[0])):
        high, low = split(values)
        lines = pl.ds(half * packed, packed)
        part = nn(high, sh_ref[lines, :]) + nn(low, sh_ref[lines, :]) + nn(high, sl_ref[lines, :])
        total = part if total is None else total + part
    high_ref[...], low_ref[...] = split(total * back_ref[0])


def square_kernel(turned_ref, high_ref, low_ref):
    high_ref[...], low_ref[...] = split(nt(turned_ref[...], turned_ref[...]))


def square(turned):
    whole = pl.BlockSpec(memory_space=pltpu.VMEM)
    return pl.pallas_call(
        square_kernel,
        out_shape=[jax.ShapeDtypeStruct(turned.shape, jnp.bfloat16)] * 2,
        in_specs=[whole],
        out_specs=[whole] * 2,
        compiler_params=pltpu.CompilerParams(vmem_limit_bytes=VMEM),
        name="square",
    )(turned)


def solve(factor, back, words, sh, sl):
    rows, packed = words.shape
    width = sh.shape[1]
    step = min(rows, 256)
    whole = pl.BlockSpec(sh.shape, lambda r: (0, 0))
    tile = pl.BlockSpec((step, width), lambda r: (r, 0))
    return pl.pallas_call(
        solve_kernel,
        out_shape=[jax.ShapeDtypeStruct((rows, width), jnp.bfloat16)] * 2,
        grid=(rows // step,),
        in_specs=[
            pl.BlockSpec(memory_space=pltpu.SMEM),
            pl.BlockSpec(memory_space=pltpu.SMEM),
            pl.BlockSpec((step, packed), lambda r: (r, 0)),
            whole,
            whole,
        ],
        out_specs=[tile, tile],
        compiler_params=pltpu.CompilerParams(vmem_limit_bytes=VMEM),
        name="solve",
    )(factor, back, words, sh, sl)


def nt(a, b):
    return lax.dot_general(a, b, (((1,), (1,)), ((), ())), preferred_element_type=jnp.float32)


def nn(a, b):
    return jnp.dot(a, b, preferred_element_type=jnp.float32)


def encode_kernel(pieces, gram_ref, even_ref, *odd_refs):
    cycle = pl.program_id(0)
    half, width = gram_ref.shape[2], gram_ref.shape[5]
    codes = encode(gram_ref[:, 0, :, 0, 0, :].reshape(2 * half, width))
    even_ref[0] = codes[:half]
    for (start, count), odd_ref in zip(pieces, odd_refs):

        @pl.when((cycle >= start) & (cycle < start + count))
        def _(odd_ref=odd_ref):
            odd_ref[0] = codes[half:]


def encode_panel(gram, panel_width, pieces, after):
    _, _, half, col_cycles = gram.shape[:4]
    packed = panel_width // 2

    def piece_spec(start, count):
        return pl.BlockSpec((1, half, packed), lambda i: (jnp.clip(i - start, 0, count - 1), 0, 0))

    kernel = functools.partial(encode_kernel, pieces)
    return pl.pallas_call(
        lambda gram_ref, *refs: kernel(gram_ref, *refs[len(after) :]),
        out_shape=[jax.ShapeDtypeStruct((n, half, packed), jnp.int32) for n in [col_cycles] + [n for _, n in pieces]],
        grid=(col_cycles,),
        in_specs=[pl.BlockSpec((2, 1, half, 1, 1, panel_width), lambda i: (i, 0, 0, 0, 0, 0))]
        + [pl.BlockSpec(memory_space=pl.ANY)] * len(after),
        out_specs=[piece_spec(0, col_cycles)] + [piece_spec(*piece) for piece in pieces],
        compiler_params=pltpu.CompilerParams(vmem_limit_bytes=VMEM),
        cost_estimate=pl.CostEstimate(flops=1, bytes_accessed=1, transcendentals=0),
        name="encode_panel",
    )(gram, *after)


def encode_rows(gram, panel_width):
    cycles, _, half = gram.shape[:3]

    def kernel(gram_ref, out_ref):
        out_ref[0] = encode(gram_ref[0, 0, :, 0, 0, :])

    return pl.pallas_call(
        kernel,
        out_shape=jax.ShapeDtypeStruct((cycles, half, panel_width // 2), jnp.int32),
        grid=(cycles,),
        in_specs=[pl.BlockSpec((1, 1, half, 1, 1, panel_width), lambda i: (i, 0, 0, 0, 0, 0))],
        out_specs=pl.BlockSpec((1, half, panel_width // 2), lambda i: (i, 0, 0)),
        compiler_params=pltpu.CompilerParams(vmem_limit_bytes=VMEM),
        name="encode_rows",
    )(gram)


def small(kernel, shape, dtype, given, after, name, blocks=None):
    specs = [pl.BlockSpec(memory_space=pltpu.SMEM if x.ndim == 1 else pltpu.VMEM) for x in given]
    count = len(given)
    return pl.pallas_call(
        lambda *refs: kernel(*refs[:count], refs[-1]),
        out_shape=jax.ShapeDtypeStruct(shape, dtype),
        in_specs=specs + [pl.BlockSpec(memory_space=pl.ANY)] * len(after),
        out_specs=pl.BlockSpec(memory_space=pltpu.VMEM),
        compiler_params=pltpu.CompilerParams(vmem_limit_bytes=VMEM),
        cost_estimate=pl.CostEstimate(flops=1, bytes_accessed=1, transcendentals=0),
        name=name,
    )(*given, *after)


def choose(first, even, start, odd, after):
    count, half, packed = odd.shape

    def kernel(first_ref, even_ref, odd_ref, *refs):
        out_ref = refs[-1]

        @pl.when(first_ref[0] == 1)
        def _():
            out_ref[...] = even_ref[...]

        @pl.when(first_ref[0] == 0)
        def _():
            out_ref[...] = odd_ref[...]

    return pl.pallas_call(
        kernel,
        out_shape=jax.ShapeDtypeStruct(odd.shape, odd.dtype),
        grid=(count // 2,),
        in_specs=[
            pl.BlockSpec(memory_space=pltpu.SMEM),
            pl.BlockSpec((2, half, packed), lambda i: (start // 2 + i, 0, 0)),
            pl.BlockSpec((2, half, packed), lambda i: (i, 0, 0)),
        ]
        + [pl.BlockSpec(memory_space=pl.ANY)] * len(after),
        out_specs=pl.BlockSpec((2, half, packed), lambda i: (i, 0, 0)),
        compiler_params=pltpu.CompilerParams(vmem_limit_bytes=VMEM),
        cost_estimate=pl.CostEstimate(flops=1, bytes_accessed=1, transcendentals=0),
        name="choose",
    )(first, even, odd, *after)


def hold(x, after):
    return pl.pallas_call(
        lambda *refs: None,
        out_shape=jax.ShapeDtypeStruct(x.shape, x.dtype),
        in_specs=[pl.BlockSpec(memory_space=pl.ANY)] * (1 + len(after)),
        out_specs=pl.BlockSpec(memory_space=pl.ANY),
        input_output_aliases={0: 0},
        cost_estimate=pl.CostEstimate(flops=1, bytes_accessed=1, transcendentals=0),
        name="hold",
    )(x, *after)


def join(arrays, after):
    def kernel(*refs):
        for k, ref in enumerate(refs[:-1]):
            refs[-1][k] = ref[...]

    return small(kernel, (len(arrays),) + arrays[0].shape, arrays[0].dtype, arrays, after, "join")


def solve_kernel(pieces, factor_ref, back_ref, first_ref, own_even_ref, even_ref, sh_ref, sl_ref, *refs):
    odds, (high_ref, low_ref) = refs[: 2 * len(pieces)], refs[-2:]
    cycle = pl.program_id(0)
    half, packed = even_ref.shape[1:]

    def solved(words):
        total = None
        for part, values in enumerate(decode(words, factor_ref[0])):
            high, low = split(values)
            lines = pl.ds(part * packed, packed)
            one = nn(high, sh_ref[lines, :]) + nn(low, sh_ref[lines, :]) + nn(high, sl_ref[lines, :])
            total = one if total is None else total + one
        high_ref[...], low_ref[...] = split(total * back_ref[0])

    own = first_ref[0] == 1
    for p, (start, count) in enumerate(pieces):

        @pl.when((cycle * 2 >= start) & (cycle * 2 < start + count))
        def _(p=p):
            rows = []
            for i in range(2):
                rows.append(jnp.where(own, own_even_ref[i], even_ref[i]))
                rows.append(jnp.where(own, odds[2 * p][i], odds[2 * p + 1][i]))
            solved(jnp.concatenate(rows, axis=0))


def solve(factor, back, first, own_even, even, odds, pieces, sh, sl, after):
    col_cycles, half, packed = even.shape
    width = sh.shape[1]
    whole = pl.BlockSpec(sh.shape, lambda r: (0, 0))
    tile = pl.BlockSpec((4 * half, width), lambda r: (r, 0))
    scalars = pl.BlockSpec(memory_space=pltpu.SMEM)
    pair = pl.BlockSpec((2, half, packed), lambda r: (r, 0, 0))

    def piece_spec(start, count):
        return pl.BlockSpec((2, half, packed), lambda r: (jnp.clip(r - start // 2, 0, count // 2 - 1), 0, 0))

    return pl.pallas_call(
        functools.partial(solve_kernel, pieces),
        out_shape=[jax.ShapeDtypeStruct((2 * col_cycles * half, width), jnp.bfloat16)] * 2,
        grid=(col_cycles // 2,),
        in_specs=[scalars] * 3
        + [pair, pair, whole, whole]
        + [piece_spec(*piece) for piece in pieces for _ in range(2)]
        + [pl.BlockSpec(memory_space=pl.ANY)] * len(after),
        out_specs=[tile, tile],
        compiler_params=pltpu.CompilerParams(vmem_limit_bytes=VMEM),
        cost_estimate=pl.CostEstimate(flops=1, bytes_accessed=1, transcendentals=0),
        name="solve",
    )(factor, back, first, own_even, even, sh, sl, *[x for pair_of in odds for x in pair_of], *after)


def solve_rows(factor, back, words, sh, sl):
    rows, packed = words.shape
    width = sh.shape[1]
    step = min(rows, 256)

    def kernel(factor_ref, back_ref, words_ref, sh_ref, sl_ref, high_ref, low_ref):
        total = None
        for part, values in enumerate(decode(words_ref[...], factor_ref[0])):
            high, low = split(values)
            lines = pl.ds(part * packed, packed)
            one = nn(high, sh_ref[lines, :]) + nn(low, sh_ref[lines, :]) + nn(high, sl_ref[lines, :])
            total = one if total is None else total + one
        high_ref[...], low_ref[...] = split(total * back_ref[0])

    whole = pl.BlockSpec(sh.shape, lambda r: (0, 0))
    tile = pl.BlockSpec((step, width), lambda r: (r, 0))
    scalars = pl.BlockSpec(memory_space=pltpu.SMEM)
    return pl.pallas_call(
        kernel,
        out_shape=[jax.ShapeDtypeStruct((rows, width), jnp.bfloat16)] * 2,
        grid=(rows // step,),
        in_specs=[scalars, scalars, pl.BlockSpec((step, packed), lambda r: (r, 0)), whole, whole],
        out_specs=[tile, tile],
        compiler_params=pltpu.CompilerParams(vmem_limit_bytes=VMEM),
        name="solve_rows",
    )(factor, back, words, sh, sl)


def update_kernel(arrays, first_cycle, step, factor_ref, places_ref, high_ref, low_ref, *refs):
    words, refs = refs[:arrays], refs[arrays:]
    gram_ref, (out_ref, ph_ref, pl_ref, in_buf, out_buf, in_sem, out_sem) = refs[0], refs[-7:]
    cycle, tile, tiles = pl.program_id(0), pl.program_id(1), pl.num_programs(1)
    index, last = cycle * tiles + tile, pl.num_programs(0) * tiles - 1
    slot = lax.rem(index, 2)
    half, packed = words[0].shape[2:]

    def part(ref, at):
        return ref.at[pl.ds(lax.rem(at, tiles) * step, step), 0, :, at // tiles + first_cycle, 0, :]

    def load(at, side):
        return pltpu.make_async_copy(part(gram_ref, at), in_buf.at[side], in_sem.at[side])

    def store(at, side):
        return pltpu.make_async_copy(out_buf.at[side], part(out_ref, at), out_sem.at[side])

    @pl.when(index == 0)
    def _():
        load(0, 0).start()

    @pl.when(index < last)
    def _():
        load(index + 1, 1 - slot).start()

    @pl.when(tile == 0)
    def _():
        base = 0
        for words_ref in words:
            def member(k, carry, words_ref=words_ref, base=base):
                a, b = decode(words_ref[k, 0], factor_ref[0])
                ah, al = split(a)
                bh, bl = split(b)
                spot = pl.ds(pl.multiple_of(places_ref[base + k] * half, half), half)
                ph_ref[spot, :packed] = ah
                ph_ref[spot, packed:] = bh
                pl_ref[spot, :packed] = al
                pl_ref[spot, packed:] = bl
                return carry

            lax.fori_loop(0, words_ref.shape[0], member, 0)
            base += words_ref.shape[0]

    count = step * half
    spot = pl.ds(pl.multiple_of(tile * count, count), count)
    high, low = high_ref[spot, :], low_ref[spot, :]
    product = nt(high, ph_ref[...]) + nt(low, ph_ref[...]) + nt(high, pl_ref[...])
    load(index, slot).wait()

    @pl.when(index >= 2)
    def _():
        store(index - 2, slot).wait()

    out_buf[slot] = in_buf[slot] - product.reshape(step, half, out_buf.shape[3])
    store(index, slot).start()

    @pl.when(index == last)
    def _():
        @pl.when(index >= 1)
        def _():
            store(index - 1, 1 - slot).wait()

        store(index, slot).wait()


def update(gram, before, factor, places, high, low, words, begin, count, first_cycle, after):
    cycles, _, half, _, _, block = gram.shape
    packed = words[0].shape[3]
    step = max(1, 512 // half)
    scalars, anywhere = pl.BlockSpec(memory_space=pltpu.SMEM), pl.BlockSpec(memory_space=pl.ANY)
    given = [factor, places, high, low, *words, gram]
    specs = [scalars, scalars] + [pl.BlockSpec(high.shape, lambda c, r: (0, 0))] * 2
    specs += [pl.BlockSpec((w.shape[0], 1, half, packed), lambda c, r: (0, c + begin, 0, 0)) for w in words]
    specs.append(anywhere)
    aliases = {}
    if before is not None:
        aliases = {len(given): 0}
        given.append(before)
        specs.append(anywhere)
    given += after
    specs += [anywhere] * len(after)
    return pl.pallas_call(
        functools.partial(update_kernel, len(words), first_cycle, step),
        out_shape=jax.ShapeDtypeStruct(gram.shape, gram.dtype),
        grid=(count, cycles // step),
        in_specs=specs,
        out_specs=anywhere,
        scratch_shapes=[pltpu.VMEM((block, 2 * packed), jnp.bfloat16)] * 2
        + [pltpu.VMEM((2, step, half, block), jnp.float32)] * 2
        + [pltpu.SemaphoreType.DMA((2,))] * 2,
        input_output_aliases=aliases,
        compiler_params=pltpu.CompilerParams(vmem_limit_bytes=VMEM),
        cost_estimate=pl.CostEstimate(flops=8 * cycles * half * count * block * 2 * packed, bytes_accessed=1, transcendentals=0),
        name="trailing_update",
    )(*given)


def gather_blocks(parts, places_ref, whole_ref):
    base = 0
    for part_ref in parts:
        size = part_ref.shape[1]

        def member(k, carry, part_ref=part_ref, base=base, size=size):
            spot = pl.ds(pl.multiple_of(places_ref[base + k] * size, size), size)
            whole_ref[spot, :] = part_ref[k]
            return carry

        lax.fori_loop(0, part_ref.shape[0], member, 0)
        base += part_ref.shape[0]


def residual_kernel(arrays, back_ref, places_ref, high_ref, low_ref, cross_ref, *refs):
    parts, (dh_ref, dl_ref, lead_ref) = refs[:arrays], refs[-3:]
    rows, half, count = cross_ref.shape[0], cross_ref.shape[2], cross_ref.shape[3]
    pl.when(pl.program_id(0) == 0)(lambda: gather_blocks(parts, places_ref, lead_ref))
    lead = lead_ref[: high_ref.shape[1], :]
    removed = nn(high_ref[...], lead) + nn(low_ref[...], lead)
    cross = cross_ref[:, 0].reshape(rows * half, count).astype(jnp.float32)
    dh_ref[...], dl_ref[...] = split(cross - removed * back_ref[0])


def residual(back, places, high, low, cross, parts, after):
    cycles, _, half, count = cross.shape
    step = max(1, 256 // half)
    panel = high.shape[1]
    scalars = pl.BlockSpec(memory_space=pltpu.SMEM)
    whole = lambda part: pl.BlockSpec(part.shape, lambda r: (0, 0, 0))
    tile = pl.BlockSpec((step * half, panel), lambda r: (r, 0))
    out = pl.BlockSpec((step * half, count), lambda r: (r, 0))
    total = sum(part.shape[0] for part in parts) * parts[0].shape[1]
    return pl.pallas_call(
        functools.partial(residual_kernel, len(parts)),
        out_shape=[jax.ShapeDtypeStruct((cycles * half, count), jnp.bfloat16)] * 2,
        grid=(cycles // step,),
        in_specs=[scalars, scalars, tile, tile, pl.BlockSpec((step, 1, half, count), lambda r: (r, 0, 0, 0))]
        + [whole(part) for part in parts]
        + [pl.BlockSpec(memory_space=pl.ANY)] * len(after),
        out_specs=[out, out],
        scratch_shapes=[pltpu.VMEM((total, count), jnp.bfloat16)],
        compiler_params=pltpu.CompilerParams(vmem_limit_bytes=VMEM),
        cost_estimate=pl.CostEstimate(flops=9 * 10**9, bytes_accessed=1, transcendentals=0),
        name="residual",
    )(back, places, high, low, cross, *parts, *after)


def rhs_kernel(arrays, places_ref, dh_ref, dl_ref, *refs):
    parts, (out_ref, lost_ref) = refs[:arrays], refs[-2:]
    pl.when(pl.program_id(0) == 0)(lambda: gather_blocks(parts, places_ref, lost_ref))
    out = nn(dh_ref[...], lost_ref[...]) + nn(dl_ref[...], lost_ref[...])
    out_ref[:, 0] = out.reshape(out_ref.shape[0], out_ref.shape[2], out.shape[1])


def rhs_step(places, dh, dl, cycles, parts, after):
    count = dh.shape[1]
    half = dh.shape[0] // cycles
    width = parts[0].shape[2]
    step = max(1, 256 // half)
    whole = lambda part: pl.BlockSpec(part.shape, lambda r: (0, 0, 0))
    tile = pl.BlockSpec((step * half, count), lambda r: (r, 0))
    return pl.pallas_call(
        functools.partial(rhs_kernel, len(parts)),
        out_shape=jax.ShapeDtypeStruct((cycles, 1, half, width), jnp.float32),
        grid=(cycles // step,),
        in_specs=[pl.BlockSpec(memory_space=pltpu.SMEM), tile, tile]
        + [whole(part) for part in parts]
        + [pl.BlockSpec(memory_space=pl.ANY)] * len(after),
        out_specs=pl.BlockSpec((step, 1, half, width), lambda r: (r, 0, 0, 0)),
        scratch_shapes=[pltpu.VMEM((count, width), jnp.bfloat16)],
        compiler_params=pltpu.CompilerParams(vmem_limit_bytes=VMEM),
        cost_estimate=pl.CostEstimate(flops=14 * 10**9, bytes_accessed=1, transcendentals=0),
        name="rhs_step",
    )(places, dh, dl, *parts, *after)


def square_kernel(turned_ref, *refs):
    high_ref, low_ref = refs[-2:]
    high_ref[...], low_ref[...] = split(nt(turned_ref[...], turned_ref[...]))


def square(turned, after):
    whole = pl.BlockSpec(memory_space=pltpu.VMEM)
    return pl.pallas_call(
        square_kernel,
        out_shape=[jax.ShapeDtypeStruct(turned.shape, jnp.bfloat16)] * 2,
        in_specs=[whole] + [pl.BlockSpec(memory_space=pl.ANY)] * len(after),
        out_specs=[whole] * 2,
        compiler_params=pltpu.CompilerParams(vmem_limit_bytes=VMEM),
        cost_estimate=pl.CostEstimate(flops=1, bytes_accessed=1, transcendentals=0),
        name="square",
    )(turned, *after)


def own_kernel(order_ref, range_ref, places_ref, rows_ref, *refs):
    out_ref = refs[-1]
    count = out_ref.shape[0]
    start = order_ref[pl.program_id(0)] * count
    any_own = (range_ref[0] < start + count) & (range_ref[1] > start)

    @pl.when(any_own)
    def _():
        shard = rows_ref.shape[0]
        lines = lax.broadcasted_iota(jnp.int32, (count, shard), 1)
        picks = jnp.where(places_ref[...] == lines, 1.0, 0.0).astype(jnp.bfloat16)
        out_ref[...] = nn(picks, rows_ref[...]).astype(jnp.bfloat16)

    @pl.when(jnp.logical_not(any_own))
    def _():
        out_ref[...] = jnp.zeros_like(out_ref)


def own_lost_rows(down_rows, places, span, order, size, after):
    shard, width = down_rows.shape
    return pl.pallas_call(
        own_kernel,
        grid_spec=pltpu.PrefetchScalarGridSpec(
            num_scalar_prefetch=2,
            grid=(order.shape[0],),
            in_specs=[
                pl.BlockSpec((size, 1), lambda i, order, span: (order[i], 0)),
                pl.BlockSpec(down_rows.shape, lambda i, order, span: (0, 0)),
                *[pl.BlockSpec(memory_space=pl.ANY)] * len(after),
            ],
            out_specs=pl.BlockSpec((size, width), lambda i, order, span: (i, 0)),
        ),
        out_shape=jax.ShapeDtypeStruct((order.shape[0] * size, width), jnp.bfloat16),
        compiler_params=pltpu.CompilerParams(vmem_limit_bytes=VMEM),
        cost_estimate=pl.CostEstimate(flops=1, bytes_accessed=1, transcendentals=0),
        name="own_lost_rows",
    )(order, span, places, down_rows, *after)


def turn(x, k):
    far = lax.axis_size("far")
    return lax.ppermute(x, "far", [(r, (r + k) % far) for r in range(far)])


def near(x):
    return lax.ppermute(x, "near", [(0, 1), (1, 0)])


def other(x):
    return lax.ppermute(x, "tp", [(0, 1), (1, 0)])


def far_order():
    far = lax.axis_size("far")
    return sorted(range(1, far), key=lambda k: min(k, far - k))


def member_at(place, flips):
    return (place * 2 + (lax.axis_index("near") ^ flips[0])) * 2 + (lax.axis_index("tp") ^ flips[1])


def spread(line, after):
    plane = [line, near(line)]
    if after:
        plane[1] = hold(plane[1], after)
    return plane + [other(x) for x in plane]


def add(a, b, after):
    def kernel(a_ref, b_ref, out_ref):
        out_ref[...] = a_ref[...] + b_ref[...]

    return small(kernel, a.shape, a.dtype, [a, b], after, "add")


def add_halves(a, b, after):
    count = a.shape[0] // 2

    def kernel(a_ref, b_ref, *refs):
        refs[-2][...] = a_ref[:count] + b_ref[:count]
        refs[-1][...] = a_ref[count:] + b_ref[count:]

    whole = pl.BlockSpec(memory_space=pltpu.VMEM)
    return pl.pallas_call(
        kernel,
        out_shape=[jax.ShapeDtypeStruct((count, a.shape[1]), a.dtype)] * 2,
        in_specs=[whole] * 2 + [pl.BlockSpec(memory_space=pl.ANY)] * len(after),
        out_specs=[whole] * 2,
        compiler_params=pltpu.CompilerParams(vmem_limit_bytes=VMEM),
        cost_estimate=pl.CostEstimate(flops=1, bytes_accessed=1, transcendentals=0),
        name="add_halves",
    )(a, b, *after)


def table(members):
    return jnp.stack(members).astype(jnp.int32)


def per_device(gram, inv_factor, cross_gram, down_rows, removed):
    cycles, _, half, col_cycles, _, block = gram.shape
    panel_width = inv_factor.shape[0]
    packed = panel_width // 2
    cols, count = lax.axis_size("col"), removed.shape[0]
    far, order = lax.axis_size("far"), far_order()
    members = lax.axis_size(MEMBERS)
    first = (lax.axis_index("col") == 0).astype(jnp.int32).reshape(1)
    here = lax.axis_index("far")
    flips = [(n, t) for t in (0, 1) for n in (0, 1)]
    around = table([member_at((here - k) % far, flip) for flip in flips for k in [0] + order])
    lined = table([member_at(z, flip) for flip in flips for z in range(far)])
    unit = LIMIT / LEVELS**2

    lead_turns = [turn(cross_gram[0, 0], k) for k in order]

    largest = jnp.max(jnp.abs(inv_factor)).astype(jnp.float32)
    scale = jnp.where(largest > 2.0**40, 2.0**-80, jnp.where(largest < 2.0**-40, 2.0**80, 1.0))
    back = jnp.where(largest > 2.0**40, 2.0**80, jnp.where(largest < 2.0**-40, 2.0**-80, 1.0)).reshape(1)
    turned = (inv_factor.astype(jnp.float32) * scale).astype(jnp.bfloat16).T
    units = jnp.full((1,), unit, jnp.float32)

    size = count // members
    places = (removed - lax.axis_index(MEMBERS) * down_rows.shape[0]).reshape(count, 1)
    span = jnp.stack([jnp.sum(places < 0), jnp.sum(places < down_rows.shape[0])]).astype(jnp.int32)
    blocks = [table([member_at(z, (n, t)) for n in (0, 1) for z in range(far)]) for t in (0, 1)]

    if cols == 2 and col_cycles == 8:
        cuts = PIECES
        even, *odds = encode_panel(gram, panel_width, cuts, [])
        to_one = lambda x: lax.ppermute(x, "col", [(0, 1)])
        got_odds = [to_one(x) for x in odds]
        last = even
    else:
        cuts = ((0, col_cycles),)
        by_cycle = encode_rows(gram, panel_width).reshape(col_cycles, cols, half, packed)
        sent = sum(lax.ppermute(by_cycle, "col", [(0, c)]) for c in range(1, cols))
        mine = jnp.where(first[0] == 1, by_cycle, sent)
        wanted = [lax.dynamic_index_in_dim(mine, lax.axis_index("col"), axis=1, keepdims=False)]
        last = by_cycle
    give = last = own_lost_rows(down_rows, places, span, blocks[1], size, [last])
    got = other(give)
    split_panel = cols == 2 and col_cycles == 8
    gathered = []

    def gather(piece):
        return lax.all_gather(piece, "far", axis=0, tiled=False)

    if split_panel:
        last = wanted = choose(first, even, cuts[0][0], got_odds[0], [last])
        gathered.append(gather(wanted))
    else:
        gathered.append(gather(wanted[0]))
    keep = last = own_lost_rows(down_rows, places, span, blocks[0], size, [last])
    if split_panel:
        for (start, _), got_odd in list(zip(cuts, got_odds))[1:]:
            last = wanted = choose(first, even, start, got_odd, [last])
            gathered.append(gather(wanted))
        got_even = to_one(hold(even, [last]))
    kept, given = add_halves(keep, got, [last])
    near_got, last = near(given), given
    if split_panel:
        sh, sl = square(turned, [last, got_even, near_got])
        high, low = solve(units, back, first, even, got_even, list(zip(odds, got_odds)), cuts, sh, sl, [])
    else:
        sh, sl = square(turned, [last])
        high, low = solve_rows(units, back, mine.reshape(cycles * half, packed), sh, sl)
    if split_panel:
        gathered[0] = hold(gathered[0], [near_got, got_even])
    lead_line = join([cross_gram[0, 0]] + lead_turns, [high])
    lead_parts = spread(lead_line, [])
    kept = add(kept, near_got, [lead_line, *gathered[1:]])
    w_own = lax.psum_scatter(kept, "far", scatter_dimension=0, tiled=True)


    dh, dl = residual(back, around, high, low, cross_gram, lead_parts, [kept])
    updated, index = None, 0
    for line, (start, n) in zip(gathered, cuts):
        arrays = spread(line, [kept if updated is None else updated])
        part = STEP if n % STEP == 0 else n
        for begin in range(0, n, part):
            after = [dh] if index == 0 else []
            updated = update(gram, updated, units * back, lined, high, low, arrays, begin, part, start + begin, after)
            if index == 0:
                w_line = lax.all_gather(hold(w_own, [updated]), "far", axis=0, tiled=False)
            if index == 2:
                w_line = hold(w_line, [updated])
            if index == 3 or n == part:
                w_parts = spread(w_line, [updated])
            index += 1
    rhs_next = rhs_step(lined, dh, dl, cycles, w_parts, [updated])
    return updated, rhs_next


def solution(mesh):
    rows, cols, tps = (mesh.shape[axis] for axis in ("row", "col", "tp"))
    cut = jax.sharding.Mesh(mesh.devices.reshape(rows // 2, 2, cols, tps), ("far", "near", "col", "tp"))
    row = ("far", "near")
    return jax.shard_map(
        per_device,
        mesh=cut,
        in_specs=(
            P(None, row, "tp", None, "col", None),
            P(),
            P(None, row, "tp", None),
            P((*row, "tp"), "col"),
            P(),
        ),
        out_specs=(P(None, row, "tp", None, "col", None), P(None, row, "tp", "col")),
        check_vma=False,
    )
```

```python
import functools

import jax
import jax.numpy as jnp
from jax import lax
from jax.experimental import pallas as pl
from jax.experimental.pallas import tpu as pltpu
from jax.sharding import PartitionSpec as P

MEMBERS = ("far", "near", "tp")
LIMIT = 24.0
LEVELS = 32767.0
VMEM = 56 * 1024 * 1024

PIECES = ((0, 4), (4, 4))
STEP = 2


def encode(values):
    root = jnp.sqrt(jnp.abs(values)) * (LEVELS / LIMIT**0.5)
    code = jnp.clip(jnp.round(jnp.where(values < 0, -root, root)), -LEVELS, LEVELS).astype(jnp.int32)
    half = values.shape[-1] // 2
    return (code[..., :half] << 16) | (code[..., half:] & 0xFFFF)


def decode(words, factor):
    upper = (words >> 16).astype(jnp.float32)
    lower = ((words << 16) >> 16).astype(jnp.float32)
    return upper * (jnp.abs(upper) * factor), lower * (jnp.abs(lower) * factor)


def split(values):
    high = values.astype(jnp.bfloat16)
    return high, (values - high.astype(jnp.float32)).astype(jnp.bfloat16)


def solve_kernel(factor_ref, back_ref, words_ref, sh_ref, sl_ref, high_ref, low_ref):
    packed = words_ref.shape[1]
    total = None
    for half, values in enumerate(decode(words_ref[...], factor_ref[0])):
        high, low = split(values)
        lines = pl.ds(half * packed, packed)
        part = nn(high, sh_ref[lines, :]) + nn(low, sh_ref[lines, :]) + nn(high, sl_ref[lines, :])
        total = part if total is None else total + part
    high_ref[...], low_ref[...] = split(total * back_ref[0])


def square_kernel(turned_ref, high_ref, low_ref):
    high_ref[...], low_ref[...] = split(nt(turned_ref[...], turned_ref[...]))


def square(turned):
    whole = pl.BlockSpec(memory_space=pltpu.VMEM)
    return pl.pallas_call(
        square_kernel,
        out_shape=[jax.ShapeDtypeStruct(turned.shape, jnp.bfloat16)] * 2,
        in_specs=[whole],
        out_specs=[whole] * 2,
        compiler_params=pltpu.CompilerParams(vmem_limit_bytes=VMEM),
        name="square",
    )(turned)


def solve(factor, back, words, sh, sl):
    rows, packed = words.shape
    width = sh.shape[1]
    step = min(rows, 256)
    whole = pl.BlockSpec(sh.shape, lambda r: (0, 0))
    tile = pl.BlockSpec((step, width), lambda r: (r, 0))
    return pl.pallas_call(
        solve_kernel,
        out_shape=[jax.ShapeDtypeStruct((rows, width), jnp.bfloat16)] * 2,
        grid=(rows // step,),
        in_specs=[
            pl.BlockSpec(memory_space=pltpu.SMEM),
            pl.BlockSpec(memory_space=pltpu.SMEM),
            pl.BlockSpec((step, packed), lambda r: (r, 0)),
            whole,
            whole,
        ],
        out_specs=[tile, tile],
        compiler_params=pltpu.CompilerParams(vmem_limit_bytes=VMEM),
        name="solve",
    )(factor, back, words, sh, sl)


def nt(a, b):
    return lax.dot_general(a, b, (((1,), (1,)), ((), ())), preferred_element_type=jnp.float32)


def nn(a, b):
    return jnp.dot(a, b, preferred_element_type=jnp.float32)


def encode_kernel(pieces, gram_ref, even_ref, *odd_refs):
    cycle = pl.program_id(0)
    half, width = gram_ref.shape[2], gram_ref.shape[5]
    codes = encode(gram_ref[:, 0, :, 0, 0, :].reshape(2 * half, width))
    even_ref[0] = codes[:half]
    for (start, count), odd_ref in zip(pieces, odd_refs):

        @pl.when((cycle >= start) & (cycle < start + count))
        def _(odd_ref=odd_ref):
            odd_ref[0] = codes[half:]


def encode_panel(gram, panel_width, pieces, after):
    _, _, half, col_cycles = gram.shape[:4]
    packed = panel_width // 2

    def piece_spec(start, count):
        return pl.BlockSpec((1, half, packed), lambda i: (jnp.clip(i - start, 0, count - 1), 0, 0))

    kernel = functools.partial(encode_kernel, pieces)
    return pl.pallas_call(
        lambda gram_ref, *refs: kernel(gram_ref, *refs[len(after) :]),
        out_shape=[jax.ShapeDtypeStruct((n, half, packed), jnp.int32) for n in [col_cycles] + [n for _, n in pieces]],
        grid=(col_cycles,),
        in_specs=[pl.BlockSpec((2, 1, half, 1, 1, panel_width), lambda i: (i, 0, 0, 0, 0, 0))]
        + [pl.BlockSpec(memory_space=pl.ANY)] * len(after),
        out_specs=[piece_spec(0, col_cycles)] + [piece_spec(*piece) for piece in pieces],
        compiler_params=pltpu.CompilerParams(vmem_limit_bytes=VMEM),
        cost_estimate=pl.CostEstimate(flops=1, bytes_accessed=1, transcendentals=0),
        name="encode_panel",
    )(gram, *after)


def encode_rows(gram, panel_width):
    cycles, _, half = gram.shape[:3]

    def kernel(gram_ref, out_ref):
        out_ref[0] = encode(gram_ref[0, 0, :, 0, 0, :])

    return pl.pallas_call(
        kernel,
        out_shape=jax.ShapeDtypeStruct((cycles, half, panel_width // 2), jnp.int32),
        grid=(cycles,),
        in_specs=[pl.BlockSpec((1, 1, half, 1, 1, panel_width), lambda i: (i, 0, 0, 0, 0, 0))],
        out_specs=pl.BlockSpec((1, half, panel_width // 2), lambda i: (i, 0, 0)),
        compiler_params=pltpu.CompilerParams(vmem_limit_bytes=VMEM),
        name="encode_rows",
    )(gram)


def small(kernel, shape, dtype, given, after, name, blocks=None):
    specs = [pl.BlockSpec(memory_space=pltpu.SMEM if x.ndim == 1 else pltpu.VMEM) for x in given]
    count = len(given)
    return pl.pallas_call(
        lambda *refs: kernel(*refs[:count], refs[-1]),
        out_shape=jax.ShapeDtypeStruct(shape, dtype),
        in_specs=specs + [pl.BlockSpec(memory_space=pl.ANY)] * len(after),
        out_specs=pl.BlockSpec(memory_space=pltpu.VMEM),
        compiler_params=pltpu.CompilerParams(vmem_limit_bytes=VMEM),
        cost_estimate=pl.CostEstimate(flops=1, bytes_accessed=1, transcendentals=0),
        name=name,
    )(*given, *after)


def choose(first, even, start, odd, after):
    count, half, packed = odd.shape

    def kernel(first_ref, even_ref, odd_ref, *refs):
        out_ref = refs[-1]

        @pl.when(first_ref[0] == 1)
        def _():
            out_ref[...] = even_ref[...]

        @pl.when(first_ref[0] == 0)
        def _():
            out_ref[...] = odd_ref[...]

    return pl.pallas_call(
        kernel,
        out_shape=jax.ShapeDtypeStruct(odd.shape, odd.dtype),
        grid=(count // 2,),
        in_specs=[
            pl.BlockSpec(memory_space=pltpu.SMEM),
            pl.BlockSpec((2, half, packed), lambda i: (start // 2 + i, 0, 0)),
            pl.BlockSpec((2, half, packed), lambda i: (i, 0, 0)),
        ]
        + [pl.BlockSpec(memory_space=pl.ANY)] * len(after),
        out_specs=pl.BlockSpec((2, half, packed), lambda i: (i, 0, 0)),
        compiler_params=pltpu.CompilerParams(vmem_limit_bytes=VMEM),
        cost_estimate=pl.CostEstimate(flops=1, bytes_accessed=1, transcendentals=0),
        name="choose",
    )(first, even, odd, *after)


def hold(x, after):
    return pl.pallas_call(
        lambda *refs: None,
        out_shape=jax.ShapeDtypeStruct(x.shape, x.dtype),
        in_specs=[pl.BlockSpec(memory_space=pl.ANY)] * (1 + len(after)),
        out_specs=pl.BlockSpec(memory_space=pl.ANY),
        input_output_aliases={0: 0},
        cost_estimate=pl.CostEstimate(flops=1, bytes_accessed=1, transcendentals=0),
        name="hold",
    )(x, *after)


def join(arrays, after):
    def kernel(*refs):
        for k, ref in enumerate(refs[:-1]):
            refs[-1][k] = ref[...]

    return small(kernel, (len(arrays),) + arrays[0].shape, arrays[0].dtype, arrays, after, "join")


def solve_kernel(pieces, factor_ref, back_ref, first_ref, own_even_ref, even_ref, sh_ref, sl_ref, *refs):
    odds, (high_ref, low_ref) = refs[: 2 * len(pieces)], refs[-2:]
    cycle = pl.program_id(0)
    half, packed = even_ref.shape[1:]

    def solved(words):
        total = None
        for part, values in enumerate(decode(words, factor_ref[0])):
            high, low = split(values)
            lines = pl.ds(part * packed, packed)
            one = nn(high, sh_ref[lines, :]) + nn(low, sh_ref[lines, :]) + nn(high, sl_ref[lines, :])
            total = one if total is None else total + one
        high_ref[...], low_ref[...] = split(total * back_ref[0])

    own = first_ref[0] == 1
    for p, (start, count) in enumerate(pieces):

        @pl.when((cycle * 2 >= start) & (cycle * 2 < start + count))
        def _(p=p):
            rows = []
            for i in range(2):
                rows.append(jnp.where(own, own_even_ref[i], even_ref[i]))
                rows.append(jnp.where(own, odds[2 * p][i], odds[2 * p + 1][i]))
            solved(jnp.concatenate(rows, axis=0))


def solve(factor, back, first, own_even, even, odds, pieces, sh, sl, after):
    col_cycles, half, packed = even.shape
    width = sh.shape[1]
    whole = pl.BlockSpec(sh.shape, lambda r: (0, 0))
    tile = pl.BlockSpec((4 * half, width), lambda r: (r, 0))
    scalars = pl.BlockSpec(memory_space=pltpu.SMEM)
    pair = pl.BlockSpec((2, half, packed), lambda r: (r, 0, 0))

    def piece_spec(start, count):
        return pl.BlockSpec((2, half, packed), lambda r: (jnp.clip(r - start // 2, 0, count // 2 - 1), 0, 0))

    return pl.pallas_call(
        functools.partial(solve_kernel, pieces),
        out_shape=[jax.ShapeDtypeStruct((2 * col_cycles * half, width), jnp.bfloat16)] * 2,
        grid=(col_cycles // 2,),
        in_specs=[scalars] * 3
        + [pair, pair, whole, whole]
        + [piece_spec(*piece) for piece in pieces for _ in range(2)]
        + [pl.BlockSpec(memory_space=pl.ANY)] * len(after),
        out_specs=[tile, tile],
        compiler_params=pltpu.CompilerParams(vmem_limit_bytes=VMEM),
        cost_estimate=pl.CostEstimate(flops=1, bytes_accessed=1, transcendentals=0),
        name="solve",
    )(factor, back, first, own_even, even, sh, sl, *[x for pair_of in odds for x in pair_of], *after)


def solve_rows(factor, back, words, sh, sl):
    rows, packed = words.shape
    width = sh.shape[1]
    step = min(rows, 256)

    def kernel(factor_ref, back_ref, words_ref, sh_ref, sl_ref, high_ref, low_ref):
        total = None
        for part, values in enumerate(decode(words_ref[...], factor_ref[0])):
            high, low = split(values)
            lines = pl.ds(part * packed, packed)
            one = nn(high, sh_ref[lines, :]) + nn(low, sh_ref[lines, :]) + nn(high, sl_ref[lines, :])
            total = one if total is None else total + one
        high_ref[...], low_ref[...] = split(total * back_ref[0])

    whole = pl.BlockSpec(sh.shape, lambda r: (0, 0))
    tile = pl.BlockSpec((step, width), lambda r: (r, 0))
    scalars = pl.BlockSpec(memory_space=pltpu.SMEM)
    return pl.pallas_call(
        kernel,
        out_shape=[jax.ShapeDtypeStruct((rows, width), jnp.bfloat16)] * 2,
        grid=(rows // step,),
        in_specs=[scalars, scalars, pl.BlockSpec((step, packed), lambda r: (r, 0)), whole, whole],
        out_specs=[tile, tile],
        compiler_params=pltpu.CompilerParams(vmem_limit_bytes=VMEM),
        name="solve_rows",
    )(factor, back, words, sh, sl)


def update_kernel(arrays, first_cycle, step, factor_ref, places_ref, high_ref, low_ref, *refs):
    words, refs = refs[:arrays], refs[arrays:]
    gram_ref, (out_ref, ph_ref, pl_ref, in_buf, out_buf, in_sem, out_sem) = refs[0], refs[-7:]
    cycle, tile, tiles = pl.program_id(0), pl.program_id(1), pl.num_programs(1)
    index, last = cycle * tiles + tile, pl.num_programs(0) * tiles - 1
    slot = lax.rem(index, 2)
    half, packed = words[0].shape[2:]

    def part(ref, at):
        return ref.at[pl.ds(lax.rem(at, tiles) * step, step), 0, :, at // tiles + first_cycle, 0, :]

    def load(at, side):
        return pltpu.make_async_copy(part(gram_ref, at), in_buf.at[side], in_sem.at[side])

    def store(at, side):
        return pltpu.make_async_copy(out_buf.at[side], part(out_ref, at), out_sem.at[side])

    @pl.when(index == 0)
    def _():
        load(0, 0).start()

    @pl.when(index < last)
    def _():
        load(index + 1, 1 - slot).start()

    @pl.when(tile == 0)
    def _():
        base = 0
        for words_ref in words:
            def member(k, carry, words_ref=words_ref, base=base):
                a, b = decode(words_ref[k, 0], factor_ref[0])
                ah, al = split(a)
                bh, bl = split(b)
                spot = pl.ds(pl.multiple_of(places_ref[base + k] * half, half), half)
                ph_ref[spot, :packed] = ah
                ph_ref[spot, packed:] = bh
                pl_ref[spot, :packed] = al
                pl_ref[spot, packed:] = bl
                return carry

            lax.fori_loop(0, words_ref.shape[0], member, 0)
            base += words_ref.shape[0]

    count = step * half
    spot = pl.ds(pl.multiple_of(tile * count, count), count)
    high, low = high_ref[spot, :], low_ref[spot, :]
    product = nt(high, ph_ref[...]) + nt(low, ph_ref[...]) + nt(high, pl_ref[...])
    load(index, slot).wait()

    @pl.when(index >= 2)
    def _():
        store(index - 2, slot).wait()

    out_buf[slot] = in_buf[slot] - product.reshape(step, half, out_buf.shape[3])
    store(index, slot).start()

    @pl.when(index == last)
    def _():
        @pl.when(index >= 1)
        def _():
            store(index - 1, 1 - slot).wait()

        store(index, slot).wait()


def update(gram, before, factor, places, high, low, words, begin, count, first_cycle, after):
    cycles, _, half, _, _, block = gram.shape
    packed = words[0].shape[3]
    step = max(1, 512 // half)
    scalars, anywhere = pl.BlockSpec(memory_space=pltpu.SMEM), pl.BlockSpec(memory_space=pl.ANY)
    given = [factor, places, high, low, *words, gram]
    specs = [scalars, scalars] + [pl.BlockSpec(high.shape, lambda c, r: (0, 0))] * 2
    specs += [pl.BlockSpec((w.shape[0], 1, half, packed), lambda c, r: (0, c + begin, 0, 0)) for w in words]
    specs.append(anywhere)
    aliases = {}
    if before is not None:
        aliases = {len(given): 0}
        given.append(before)
        specs.append(anywhere)
    given += after
    specs += [anywhere] * len(after)
    return pl.pallas_call(
        functools.partial(update_kernel, len(words), first_cycle, step),
        out_shape=jax.ShapeDtypeStruct(gram.shape, gram.dtype),
        grid=(count, cycles // step),
        in_specs=specs,
        out_specs=anywhere,
        scratch_shapes=[pltpu.VMEM((block, 2 * packed), jnp.bfloat16)] * 2
        + [pltpu.VMEM((2, step, half, block), jnp.float32)] * 2
        + [pltpu.SemaphoreType.DMA((2,))] * 2,
        input_output_aliases=aliases,
        compiler_params=pltpu.CompilerParams(vmem_limit_bytes=VMEM),
        cost_estimate=pl.CostEstimate(flops=8 * cycles * half * count * block * 2 * packed, bytes_accessed=1, transcendentals=0),
        name="trailing_update",
    )(*given)


def gather_blocks(parts, places_ref, whole_ref):
    base = 0
    for part_ref in parts:
        size = part_ref.shape[1]

        def member(k, carry, part_ref=part_ref, base=base, size=size):
            spot = pl.ds(pl.multiple_of(places_ref[base + k] * size, size), size)
            whole_ref[spot, :] = part_ref[k]
            return carry

        lax.fori_loop(0, part_ref.shape[0], member, 0)
        base += part_ref.shape[0]


def residual_kernel(arrays, back_ref, places_ref, high_ref, low_ref, cross_ref, *refs):
    parts, (dh_ref, dl_ref, lead_ref) = refs[:arrays], refs[-3:]
    rows, half, count = cross_ref.shape[0], cross_ref.shape[2], cross_ref.shape[3]
    pl.when(pl.program_id(0) == 0)(lambda: gather_blocks(parts, places_ref, lead_ref))
    lead = lead_ref[: high_ref.shape[1], :]
    removed = nn(high_ref[...], lead) + nn(low_ref[...], lead)
    cross = cross_ref[:, 0].reshape(rows * half, count).astype(jnp.float32)
    dh_ref[...], dl_ref[...] = split(cross - removed * back_ref[0])


def residual(back, places, high, low, cross, parts, after):
    cycles, _, half, count = cross.shape
    step = max(1, 256 // half)
    panel = high.shape[1]
    scalars = pl.BlockSpec(memory_space=pltpu.SMEM)
    whole = lambda part: pl.BlockSpec(part.shape, lambda r: (0, 0, 0))
    tile = pl.BlockSpec((step * half, panel), lambda r: (r, 0))
    out = pl.BlockSpec((step * half, count), lambda r: (r, 0))
    total = sum(part.shape[0] for part in parts) * parts[0].shape[1]
    return pl.pallas_call(
        functools.partial(residual_kernel, len(parts)),
        out_shape=[jax.ShapeDtypeStruct((cycles * half, count), jnp.bfloat16)] * 2,
        grid=(cycles // step,),
        in_specs=[scalars, scalars, tile, tile, pl.BlockSpec((step, 1, half, count), lambda r: (r, 0, 0, 0))]
        + [whole(part) for part in parts]
        + [pl.BlockSpec(memory_space=pl.ANY)] * len(after),
        out_specs=[out, out],
        scratch_shapes=[pltpu.VMEM((total, count), jnp.bfloat16)],
        compiler_params=pltpu.CompilerParams(vmem_limit_bytes=VMEM),
        cost_estimate=pl.CostEstimate(flops=9 * 10**9, bytes_accessed=1, transcendentals=0),
        name="residual",
    )(back, places, high, low, cross, *parts, *after)


def rhs_kernel(arrays, places_ref, dh_ref, dl_ref, *refs):
    parts, (out_ref, lost_ref) = refs[:arrays], refs[-2:]
    pl.when(pl.program_id(0) == 0)(lambda: gather_blocks(parts, places_ref, lost_ref))
    out = nn(dh_ref[...], lost_ref[...]) + nn(dl_ref[...], lost_ref[...])
    out_ref[:, 0] = out.reshape(out_ref.shape[0], out_ref.shape[2], out.shape[1])


def rhs_step(places, dh, dl, cycles, parts, after):
    count = dh.shape[1]
    half = dh.shape[0] // cycles
    width = parts[0].shape[2]
    step = max(1, 256 // half)
    whole = lambda part: pl.BlockSpec(part.shape, lambda r: (0, 0, 0))
    tile = pl.BlockSpec((step * half, count), lambda r: (r, 0))
    return pl.pallas_call(
        functools.partial(rhs_kernel, len(parts)),
        out_shape=jax.ShapeDtypeStruct((cycles, 1, half, width), jnp.float32),
        grid=(cycles // step,),
        in_specs=[pl.BlockSpec(memory_space=pltpu.SMEM), tile, tile]
        + [whole(part) for part in parts]
        + [pl.BlockSpec(memory_space=pl.ANY)] * len(after),
        out_specs=pl.BlockSpec((step, 1, half, width), lambda r: (r, 0, 0, 0)),
        scratch_shapes=[pltpu.VMEM((count, width), jnp.bfloat16)],
        compiler_params=pltpu.CompilerParams(vmem_limit_bytes=VMEM),
        cost_estimate=pl.CostEstimate(flops=14 * 10**9, bytes_accessed=1, transcendentals=0),
        name="rhs_step",
    )(places, dh, dl, *parts, *after)


def square_kernel(turned_ref, *refs):
    high_ref, low_ref = refs[-2:]
    high_ref[...], low_ref[...] = split(nt(turned_ref[...], turned_ref[...]))


def square(turned, after):
    whole = pl.BlockSpec(memory_space=pltpu.VMEM)
    return pl.pallas_call(
        square_kernel,
        out_shape=[jax.ShapeDtypeStruct(turned.shape, jnp.bfloat16)] * 2,
        in_specs=[whole] + [pl.BlockSpec(memory_space=pl.ANY)] * len(after),
        out_specs=[whole] * 2,
        compiler_params=pltpu.CompilerParams(vmem_limit_bytes=VMEM),
        cost_estimate=pl.CostEstimate(flops=1, bytes_accessed=1, transcendentals=0),
        name="square",
    )(turned, *after)


def own_kernel(order_ref, range_ref, places_ref, rows_ref, *refs):
    out_ref = refs[-1]
    count = out_ref.shape[0]
    start = order_ref[pl.program_id(0)] * count
    any_own = (range_ref[0] < start + count) & (range_ref[1] > start)

    @pl.when(any_own)
    def _():
        shard = rows_ref.shape[0]
        lines = lax.broadcasted_iota(jnp.int32, (count, shard), 1)
        picks = jnp.where(places_ref[...] == lines, 1.0, 0.0).astype(jnp.bfloat16)
        out_ref[...] = nn(picks, rows_ref[...]).astype(jnp.bfloat16)

    @pl.when(jnp.logical_not(any_own))
    def _():
        out_ref[...] = jnp.zeros_like(out_ref)


def own_lost_rows(down_rows, places, span, order, size, after):
    shard, width = down_rows.shape
    return pl.pallas_call(
        own_kernel,
        grid_spec=pltpu.PrefetchScalarGridSpec(
            num_scalar_prefetch=2,
            grid=(order.shape[0],),
            in_specs=[
                pl.BlockSpec((size, 1), lambda i, order, span: (order[i], 0)),
                pl.BlockSpec(down_rows.shape, lambda i, order, span: (0, 0)),
                *[pl.BlockSpec(memory_space=pl.ANY)] * len(after),
            ],
            out_specs=pl.BlockSpec((size, width), lambda i, order, span: (i, 0)),
        ),
        out_shape=jax.ShapeDtypeStruct((order.shape[0] * size, width), jnp.bfloat16),
        compiler_params=pltpu.CompilerParams(vmem_limit_bytes=VMEM),
        cost_estimate=pl.CostEstimate(flops=1, bytes_accessed=1, transcendentals=0),
        name="own_lost_rows",
    )(order, span, places, down_rows, *after)


def turn(x, k):
    far = lax.axis_size("far")
    return lax.ppermute(x, "far", [(r, (r + k) % far) for r in range(far)])


def near(x):
    return lax.ppermute(x, "near", [(0, 1), (1, 0)])


def other(x):
    return lax.ppermute(x, "tp", [(0, 1), (1, 0)])


def far_order():
    far = lax.axis_size("far")
    return sorted(range(1, far), key=lambda k: min(k, far - k))


def member_at(place, flips):
    return (place * 2 + (lax.axis_index("near") ^ flips[0])) * 2 + (lax.axis_index("tp") ^ flips[1])


def spread(line, after):
    plane = [line, near(line)]
    if after:
        plane[1] = hold(plane[1], after)
    return plane + [other(x) for x in plane]


def others_of(line, here):
    far = line.shape[0]
    order = jnp.stack([(here - k) % far for k in range(1, far)]).astype(jnp.int32)

    def kernel(order_ref, line_ref, out_ref):
        out_ref[...] = line_ref[...]

    return pl.pallas_call(
        kernel,
        grid_spec=pltpu.PrefetchScalarGridSpec(
            num_scalar_prefetch=1,
            grid=(far - 1,),
            in_specs=[pl.BlockSpec((1, *line.shape[1:]), lambda i, order: (order[i], 0, 0, 0))],
            out_specs=pl.BlockSpec((1, *line.shape[1:]), lambda i, order: (i, 0, 0, 0)),
        ),
        out_shape=jax.ShapeDtypeStruct((far - 1, *line.shape[1:]), line.dtype),
        compiler_params=pltpu.CompilerParams(vmem_limit_bytes=VMEM),
        cost_estimate=pl.CostEstimate(flops=1, bytes_accessed=1, transcendentals=0),
        name="others_of",
    )(order, line)


def add(a, b, after):
    def kernel(a_ref, b_ref, out_ref):
        out_ref[...] = a_ref[...] + b_ref[...]

    return small(kernel, a.shape, a.dtype, [a, b], after, "add")


def add_halves(a, b, after):
    count = a.shape[0] // 2

    def kernel(a_ref, b_ref, *refs):
        refs[-2][...] = a_ref[:count] + b_ref[:count]
        refs[-1][...] = a_ref[count:] + b_ref[count:]

    whole = pl.BlockSpec(memory_space=pltpu.VMEM)
    return pl.pallas_call(
        kernel,
        out_shape=[jax.ShapeDtypeStruct((count, a.shape[1]), a.dtype)] * 2,
        in_specs=[whole] * 2 + [pl.BlockSpec(memory_space=pl.ANY)] * len(after),
        out_specs=[whole] * 2,
        compiler_params=pltpu.CompilerParams(vmem_limit_bytes=VMEM),
        cost_estimate=pl.CostEstimate(flops=1, bytes_accessed=1, transcendentals=0),
        name="add_halves",
    )(a, b, *after)


def table(members):
    return jnp.stack(members).astype(jnp.int32)


def per_device(gram, inv_factor, cross_gram, down_rows, removed):
    cycles, _, half, col_cycles, _, block = gram.shape
    panel_width = inv_factor.shape[0]
    packed = panel_width // 2
    cols, count = lax.axis_size("col"), removed.shape[0]
    far, order = lax.axis_size("far"), far_order()
    members = lax.axis_size(MEMBERS)
    first = (lax.axis_index("col") == 0).astype(jnp.int32).reshape(1)
    here = lax.axis_index("far")
    flips = [(n, t) for t in (0, 1) for n in (0, 1)]
    around = table([member_at((here - k) % far, flip) for flip in flips for k in [0] + order])
    lined = table([member_at(z, flip) for flip in flips for z in range(far)])
    unit = LIMIT / LEVELS**2

    lead_turns = [turn(cross_gram[0, 0], k) for k in order]

    largest = jnp.max(jnp.abs(inv_factor)).astype(jnp.float32)
    scale = jnp.where(largest > 2.0**40, 2.0**-80, jnp.where(largest < 2.0**-40, 2.0**80, 1.0))
    back = jnp.where(largest > 2.0**40, 2.0**80, jnp.where(largest < 2.0**-40, 2.0**-80, 1.0)).reshape(1)
    turned = (inv_factor.astype(jnp.float32) * scale).astype(jnp.bfloat16).T
    units = jnp.full((1,), unit, jnp.float32)

    size = count // members
    places = (removed - lax.axis_index(MEMBERS) * down_rows.shape[0]).reshape(count, 1)
    span = jnp.stack([jnp.sum(places < 0), jnp.sum(places < down_rows.shape[0])]).astype(jnp.int32)
    blocks = [table([member_at(z, (n, t)) for n in (0, 1) for z in range(far)]) for t in (0, 1)]

    if cols == 2 and col_cycles == 8:
        cuts = PIECES
        even, *odds = encode_panel(gram, panel_width, cuts, [])
        to_one = lambda x: lax.ppermute(x, "col", [(0, 1)])
        got_odds = [to_one(x) for x in odds]
        last = even
    else:
        cuts = ((0, col_cycles),)
        by_cycle = encode_rows(gram, panel_width).reshape(col_cycles, cols, half, packed)
        sent = sum(lax.ppermute(by_cycle, "col", [(0, c)]) for c in range(1, cols))
        mine = jnp.where(first[0] == 1, by_cycle, sent)
        wanted = [lax.dynamic_index_in_dim(mine, lax.axis_index("col"), axis=1, keepdims=False)]
        last = by_cycle
    give = last = own_lost_rows(down_rows, places, span, blocks[1], size, [last])
    got = other(give)
    split_panel = cols == 2 and col_cycles == 8
    gathered = []

    def gather(piece):
        return lax.all_gather(piece, "far", axis=0, tiled=False)

    if split_panel:
        last = wanted = choose(first, even, cuts[0][0], got_odds[0], [last])
        gathered.append(gather(wanted))
        beside = [near(wanted)]
    else:
        gathered.append(gather(wanted[0]))
    keep = last = own_lost_rows(down_rows, places, span, blocks[0], size, [last])
    if split_panel:
        for (start, _), got_odd in list(zip(cuts, got_odds))[1:]:
            last = wanted = choose(first, even, start, got_odd, [last])
            gathered.append(gather(wanted))
            beside.append(near(wanted))
        got_even = to_one(hold(even, [last]))
    kept, given = add_halves(keep, got, [last, beside[0]] if split_panel else [last])
    near_got, last = near(given), given
    if split_panel:
        sh, sl = square(turned, [last, got_even, near_got])
        high, low = solve(units, back, first, even, got_even, list(zip(odds, got_odds)), cuts, sh, sl, [])
    else:
        sh, sl = square(turned, [last])
        high, low = solve_rows(units, back, mine.reshape(cycles * half, packed), sh, sl)
    if split_panel:
        gathered[0] = hold(gathered[0], [near_got, got_even])
    lead_line = join([cross_gram[0, 0]] + lead_turns, [high])
    kept = add(kept, near_got, [lead_line, *gathered[1:], *(beside[1:] if split_panel else [])])
    w_own = lax.psum_scatter(kept, "far", scatter_dimension=0, tiled=True)


    updated, index, panel_places = None, 0, lined
    if split_panel:
        places = []
        for t in (0, 1):
            places += [member_at(z, (0, t)) for z in range(far)]
            places += [member_at((here - k) % far, (1, t)) for k in range(far)]
        panel_places = table(places)
    for piece, (line, (start, n)) in enumerate(zip(gathered, cuts)):
        last = kept if updated is None else updated
        if split_panel:
            arrays = [line, beside[piece][None], hold(near(others_of(line, here)), [last])]
            arrays += [other(x) for x in arrays]
        else:
            arrays = spread(line, [last])
        part = STEP if n % STEP == 0 else n
        for begin in range(0, n, part):
            after = [kept] if index == 0 else [dh] if index == 2 else []
            updated = update(gram, updated, units * back, panel_places, high, low, arrays, begin, part, start + begin, after)
            if index == 0:
                lead_parts = spread(lead_line, [updated])
                w_line = lax.all_gather(hold(w_own, [updated]), "far", axis=0, tiled=False)
            if index == 1 or n == part:
                dh, dl = residual(back, around, high, low, cross_gram, lead_parts, [updated])
            if index == 2:
                w_line = hold(w_line, [updated])
            if index == 3 or n == part:
                w_parts = spread(w_line, [updated])
            index += 1
    rhs_next = rhs_step(lined, dh, dl, cycles, w_parts, [updated])
    return updated, rhs_next


def solution(mesh):
    rows, cols, tps = (mesh.shape[axis] for axis in ("row", "col", "tp"))
    cut = jax.sharding.Mesh(mesh.devices.reshape(rows // 2, 2, cols, tps), ("far", "near", "col", "tp"))
    row = ("far", "near")
    return jax.shard_map(
        per_device,
        mesh=cut,
        in_specs=(
            P(None, row, "tp", None, "col", None),
            P(),
            P(None, row, "tp", None),
            P((*row, "tp"), "col"),
            P(),
        ),
        out_specs=(P(None, row, "tp", None, "col", None), P(None, row, "tp", "col")),
        check_vma=False,
    )
```
